32 devices in a mesh: gx: 2 (over x), gy: 4 (over y, core), gz: 4 (over z).
Axes of the slice: x: 2, y: 2, z: 4, core: 2. Of those that a mesh axis runs over, the one named last changes fastest.
Arguments:
- residual: bfloat16 [2, 4, 4, 6, 32, 512], P('gx', 'gy', 'gz'), may hold values from -6 to 6
- panel: bfloat16 [2, 4, 4, 6, 1024, 512], P('gx', 'gy', 'gz'), may hold values from -0.1875 to 0.1875
- face_block: bfloat16 [2, 4, 4, 6, 512, 512], P('gx', 'gy', 'gz'), may hold values from -0.25 to 0.25
- deluxe_inv: bfloat16 [2, 4, 4, 6, 512, 512], P('gx', 'gy', 'gz'), may hold values from -0.25 to 0.25
- basis: bfloat16 [2, 4, 4, 6, 24, 512], P('gx', 'gy', 'gz'), may hold values from -0.25 to 0.25
- face_size: int32 [2, 4, 4, 6], P('gx', 'gy', 'gz'), may hold values from 128 to 512, as said below
- coarse_idx: int32 [2, 4, 4, 6, 24], P('gx', 'gy', 'gz'), may hold values from 0 to 63, as said below
- coarse_scale: float32 [2, 4, 4, 32], P('gx', 'gy', 'gz'), may hold values from 0.5 to 4
Outputs:
- corrected: bfloat16 [2, 4, 4, 6, 32, 512], P('gx', 'gy', 'gz')
The draws below stay inside these ranges and needn't reach their ends.
Inputs may be any that keep to these rules, and one draw needn't show every extreme that they name: `face_size`: A face has the same size on both of its slots; the largest face holds all 512 positions and the smallest a quarter of them. `coarse_idx`: the 24 entries of one slot are distinct.
All inputs are finite; a program needn't handle non-finite values.
Results may differ from the reference program's by a relative error of at most 0.0064.
Values sent between devices are 32-bit elements; how exact they have to be, the bound alone decides.
A program may use at most 64 MiB of HBM per device.

```python
import math
import jax
import jax.numpy as jnp
from jax import lax

F = 512
K = 1024
NR = 32
CO_DEV = 32
NCB = 24
BX = 2
BY = 4
BZ = 4


def draw_face_size(key, part):
    key = jax.random.fold_in(key, 11)
    first, second, third = jax.random.split(key, 3)
    size_x = jax.random.randint(first, (BX, BY, BZ), F // 4, F + 1).astype(jnp.int32)
    size_y = jax.random.randint(second, (BX, BY, BZ), F // 4, F + 1).astype(jnp.int32)
    size_z = jax.random.randint(third, (BX, BY, BZ), F // 4, F + 1).astype(jnp.int32)
    size_x = size_x.at[0, 0, 0].set(F)
    size_y = size_y.at[0, 0, 0].set(F // 4)
    return jnp.stack([size_x, jnp.roll(size_x, 1, 0), size_y, jnp.roll(size_y, 1, 1), size_z, jnp.roll(size_z, 1, 2)], axis=-1)


def draw_coarse_idx(key, part):
    key = jax.random.fold_in(key, 23)
    keys = jax.random.split(key, BX * BY * BZ * 6)
    chosen = jax.vmap(lambda single: jax.random.permutation(single, 2 * CO_DEV)[:NCB])(keys)
    chosen = chosen.reshape((BX, BY, BZ, 6, NCB)).astype(jnp.int32)
    ramp = jnp.arange(NCB, dtype=jnp.int32)
    chosen = chosen.at[0, 0, 0, 0].set(2 * CO_DEV - 1 - ramp)
    chosen = chosen.at[0, 0, 0, 5].set(ramp)
    return chosen


def block_levels(key, dims, shards, least, high):
    def one(axis_at, parts):
        heights = jax.random.uniform(jax.random.fold_in(jax.random.fold_in(key, 6), axis_at), (parts,), jnp.float32, least / len(shards), high / len(shards))
        return jnp.repeat(jnp.exp(heights), dims[axis_at] // parts).reshape((-1,) + (1,) * (len(dims) - axis_at - 1))

    gain = one(*shards[0])
    for cut in shards[1:]:
        gain = gain * one(*cut)
    return gain


def scatter_about(key, shape, spread, bound, cuts=(), held_as=jnp.bfloat16):
    values = spread * jax.random.normal(key, shape, jnp.float32)
    if cuts:
        values = values * block_levels(key, shape, cuts, -0.22, 0.18)
    return jnp.clip(values, -bound, bound).astype(held_as)


def setup_inputs(seed: int = 0) -> dict:
    seeds = jax.random.split(jax.random.key(seed), 9)
    residual = scatter_about(seeds[0], (BX, BY, BZ, 6, NR, F), 1.0, 6.0, ((0, 2), (1, 4), (2, 4)))
    panel = scatter_about(seeds[1], (BX, BY, BZ, 6, K, F), K ** -0.5, 0.1875, ((0, 2), (1, 4), (2, 4)))
    face_block = scatter_about(seeds[2], (BX, BY, BZ, 6, F, F), F ** -0.5, 0.25, ((0, 2), (1, 4), (2, 4)))
    deluxe_inv = scatter_about(seeds[3], (BX, BY, BZ, 6, F, F), F ** -0.5, 0.25, ((0, 2), (1, 4), (2, 4)))
    basis = scatter_about(seeds[4], (BX, BY, BZ, 6, NCB, F), F ** -0.5, 0.25, ((0, 2), (1, 4), (2, 4)))
    face_size = draw_face_size(jax.random.fold_in(seeds[8], 71), 0)
    coarse_idx = draw_coarse_idx(jax.random.fold_in(seeds[8], 71), 0)
    coarse_scale = jnp.clip(jnp.exp(math.log(4.0) - 2.0794415 * jax.random.uniform(seeds[7], (BX, BY, BZ, CO_DEV), jnp.float32) ** block_levels(seeds[7], (BX, BY, BZ, CO_DEV), ((0, 2), (1, 4), (2, 4)), -0.2, 0.2)), 0.5, 4.0)
    return dict(residual=residual, panel=panel, face_block=face_block, deluxe_inv=deluxe_inv, basis=basis, face_size=face_size, coarse_idx=coarse_idx, coarse_scale=coarse_scale)


def partner_roll(values):
    return jnp.stack([jnp.roll(values[:, :, :, 1], -1, 0), jnp.roll(values[:, :, :, 0], 1, 0),
                      jnp.roll(values[:, :, :, 3], -1, 1), jnp.roll(values[:, :, :, 2], 1, 1),
                      jnp.roll(values[:, :, :, 5], -1, 2), jnp.roll(values[:, :, :, 4], 1, 2)], axis=3)


def local_apply(operands):
    pieces, blocks, values, facemask = operands
    wide = pieces.astype(jnp.float32)
    inner = jnp.einsum("skf,skg->sfg", wide, wide)
    schur = (blocks.astype(jnp.float32) - inner).astype(jnp.bfloat16)
    masked = (values.astype(jnp.float32) * facemask[:, None, :]).astype(jnp.bfloat16)
    applied = jnp.einsum("srf,sgf->srg", masked.astype(jnp.float32), schur.astype(jnp.float32))
    return applied * facemask[:, None, :]


def local_average(operands):
    summed, inverses, facemask = operands
    averaged = jnp.einsum("srf,sgf->srg", summed.astype(jnp.float32), inverses.astype(jnp.float32))
    return (averaged * facemask[:, None, :]).astype(jnp.bfloat16)


def reference(residual, panel, face_block, deluxe_inv, basis, face_size, coarse_idx, coarse_scale):
    blocks_all = BX * BY * BZ
    facemask = (jnp.arange(F, dtype=jnp.int32)[None, None, None, None, :] < face_size[..., None]).astype(jnp.float32)

    def flatten(array):
        return array.reshape((blocks_all,) + array.shape[3:])

    applied = lax.map(local_apply, (flatten(panel), flatten(face_block), flatten(residual), flatten(facemask)))
    applied = applied.reshape((BX, BY, BZ, 6, NR, F))
    summed = (applied + partner_roll(applied)).astype(jnp.bfloat16)
    averaged = lax.map(local_average, (flatten(summed), flatten(deluxe_inv), flatten(facemask)))
    averaged = averaged.reshape((BX, BY, BZ, 6, NR, F))
    basis_wide = basis.astype(jnp.float32)
    partial_value = jnp.einsum("xyzsrf,xyzscf->xyzscr", averaged.astype(jnp.float32), basis_wide,
                         precision=lax.Precision.HIGHEST)
    linear = jnp.arange(blocks_all, dtype=jnp.int32).reshape((BX, BY, BZ))
    neighbour = partner_roll(jnp.broadcast_to(linear[:, :, :, None], (BX, BY, BZ, 6)))
    global_idx = jnp.where(coarse_idx < CO_DEV, linear[:, :, :, None, None] * CO_DEV + coarse_idx,
                           neighbour[..., None] * CO_DEV + coarse_idx - CO_DEV).astype(jnp.int32)
    coarse = jax.ops.segment_sum(partial_value.reshape((-1, NR)), global_idx.reshape(-1),
                                 num_segments=blocks_all * CO_DEV)
    correction = coarse * coarse_scale.reshape(-1)[:, None]
    picked = correction[global_idx]
    added = jnp.einsum("xyzscr,xyzscf->xyzsrf", picked, basis_wide, precision=lax.Precision.HIGHEST)
    corrected = (averaged.astype(jnp.float32) + added) * facemask[:, :, :, :, None, :]
    return corrected.astype(jnp.bfloat16)
```

```python
import functools

import jax
import jax.numpy as jnp
from jax import lax
from jax.experimental import pallas as pl
from jax.experimental.pallas import tpu as pltpu
from jax.sharding import PartitionSpec as P

AXES = ("gx", "gy", "gz")
ORDER = (0, 1, 4, 5, 2, 3)
MESH = pl.DeviceIdType.MESH
F32 = jnp.float32
BF16 = jnp.bfloat16


def dot_nt(a, b):
    return lax.dot_general(a, b, (((1,), (1,)), ((), ())), preferred_element_type=F32)


def dot_nn(a, b):
    return lax.dot_general(a, b, (((1,), (0,)), ((), ())), preferred_element_type=F32)


def kernel(
    sizes,
    residual, panel, face_block, deluxe_inv, basis, size_ref, idx_ref, scale_ref,
    out_ref,
    res_v, pan_v, fb_v, inv_v, bas_v, size_s, idx_v, scale_v,
    expanded, applied, recv1, averaged, send2, recv2, send3, recv3,
    sem_res, sem_pan, sem_fb, sem_inv, sem_bas, sem_small,
    ssem1, rsem1, ssem2, rsem2, ssem3, rsem3,
):
    me = [lax.axis_index(name) for name in AXES]

    def neighbour(slot):
        axis = slot // 2
        step = 1 if slot % 2 == 0 else sizes[axis] - 1
        coords = list(me)
        coords[axis] = lax.rem(me[axis] + step, sizes[axis])
        return tuple(coords)

    barrier = pltpu.get_barrier_semaphore()
    for slot in range(6):
        pl.semaphore_signal(barrier, inc=1, device_id=neighbour(slot), device_id_type=MESH)

    def remote(src, dst, ssem, rsem, slot):
        return pltpu.make_async_remote_copy(
            src_ref=src.at[slot] if src.shape[0] == 6 else src.at[0],
            dst_ref=dst.at[slot ^ 1],
            send_sem=ssem.at[slot],
            recv_sem=rsem.at[slot ^ 1],
            device_id=neighbour(slot),
            device_id_type=MESH,
        )

    c_size = pltpu.make_async_copy(size_ref.at[0, 0], size_s, sem_small.at[0])
    c_idx = pltpu.make_async_copy(idx_ref.at[0, 0, 0], idx_v, sem_small.at[1])
    c_scale = pltpu.make_async_copy(scale_ref.at[0, 0], scale_v, sem_small.at[2])
    c_res = pltpu.make_async_copy(residual.at[0, 0, 0], res_v, sem_res)
    c_bas = pltpu.make_async_copy(basis.at[0, 0, 0], bas_v, sem_bas)
    c_pan = [pltpu.make_async_copy(panel.at[0, 0, 0, s], pan_v.at[s], sem_pan.at[s]) for s in range(6)]
    c_fb = [pltpu.make_async_copy(face_block.at[0, 0, 0, s], fb_v.at[s], sem_fb.at[s]) for s in range(6)]
    c_inv = [pltpu.make_async_copy(deluxe_inv.at[0, 0, 0, s], inv_v.at[s], sem_inv.at[s]) for s in range(6)]
    for copy in (c_size, c_idx, c_scale, c_res, c_bas):
        copy.start()
    for s in ORDER:
        c_pan[s].start()
        c_fb[s].start()
    for s in ORDER:
        c_inv[s].start()

    width = res_v.shape[-1]
    lane = lax.broadcasted_iota(jnp.int32, (1, width), 1)
    c_size.wait()
    live = [lane < size_s[0, s] for s in range(6)]

    c_idx.wait()
    c_bas.wait()
    row = lax.broadcasted_iota(jnp.int32, (256, 1), 0)
    unknown = (row & 31) + 32 * (row >> 7)
    for s in ORDER:
        onehot = jnp.where(unknown == idx_v[pl.ds(s, 1), :], 1.0, 0.0).astype(BF16)
        expanded[s] = dot_nn(onehot, bas_v[s]).astype(BF16)

    c_res.wait()
    for k, s in enumerate(ORDER):
        c_pan[s].wait()
        masked = jnp.where(live[s], res_v[s].astype(F32), 0.0).astype(BF16)
        inner = dot_nt(masked, pan_v[s]).astype(BF16)
        through = dot_nn(inner, pan_v[s])
        c_fb[s].wait()
        value = dot_nt(masked, fb_v[s]) - through
        applied[s] = jnp.where(live[s], value, 0.0)
        if k == 0:
            pl.semaphore_wait(barrier, 6)
        remote(applied, recv1, ssem1, rsem1, s).start()

    group8 = lax.broadcasted_iota(jnp.int32, (8, 128), 1) >> 5

    def packed(wide):
        total = jnp.where(group8 == 0, wide[0:8], 0.0)
        for j in range(1, 4):
            total = jnp.where(group8 == j, wide[8 * j:8 * j + 8], total)
        return total

    def spread(tile):
        return jnp.concatenate([jnp.where(group8 == j, tile, 0.0) for j in range(4)], axis=0)

    own = jnp.zeros((8, 128), F32)
    for s in ORDER:
        remote(applied, recv1, ssem1, rsem1, s ^ 1).wait_recv()
        c_inv[s].wait()
        summed = (applied[s] + recv1[s]).astype(BF16)
        value = jnp.where(live[s], dot_nt(summed, inv_v[s]), 0.0).astype(BF16)
        averaged[s] = value
        split = dot_nt(value, expanded[s])
        own = own + packed(split[:, 0:128])
        send2[s] = packed(split[:, 128:256])
        remote(send2, recv2, ssem2, rsem2, s).start()

    c_scale.wait()
    scale = jnp.concatenate([scale_v[...]] * 4, axis=1)
    for s in ORDER:
        remote(send2, recv2, ssem2, rsem2, s ^ 1).wait_recv()
        own = own + recv2[s]
    correction = own * scale
    send3[0] = correction
    for s in ORDER:
        remote(send3, recv3, ssem3, rsem3, s).start()

    def halves(tile):
        high = tile.astype(BF16)
        return high, (tile - high.astype(F32)).astype(BF16)

    mine = spread(correction)
    for s in ORDER:
        remote(send3, recv3, ssem3, rsem3, s ^ 1).wait_recv()
        table = jnp.concatenate([mine, spread(recv3[s])], axis=1)
        high, low = halves(table)
        added = dot_nn(high, expanded[s]) + dot_nn(low, expanded[s])
        out_ref[0, 0, 0, s] = jnp.where(live[s], averaged[s].astype(F32) + added, 0.0).astype(BF16)

    for s in ORDER:
        remote(applied, recv1, ssem1, rsem1, s).wait_send()
        remote(send2, recv2, ssem2, rsem2, s).wait_send()
        remote(send3, recv3, ssem3, rsem3, s).wait_send()


def on_device(sizes, residual, panel, face_block, deluxe_inv, basis, face_size, coarse_idx, coarse_scale):
    slots, rows, width = residual.shape[3:]
    depth = panel.shape[4]
    entries = basis.shape[4]
    owned = coarse_scale.shape[-1]
    dma = pltpu.SemaphoreType.DMA
    return pl.pallas_call(
        functools.partial(kernel, sizes),
        out_shape=jax.ShapeDtypeStruct(residual.shape, BF16),
        in_specs=[pl.BlockSpec(memory_space=pl.ANY)] * 8,
        out_specs=pl.BlockSpec(memory_space=pltpu.VMEM),
        scratch_shapes=[
            pltpu.VMEM((slots, rows, width), BF16),
            pltpu.VMEM((slots, depth, width), BF16),
            pltpu.VMEM((slots, width, width), BF16),
            pltpu.VMEM((slots, width, width), BF16),
            pltpu.VMEM((slots, entries, width), BF16),
            pltpu.SMEM((1, slots), jnp.int32),
            pltpu.VMEM((slots, entries), jnp.int32),
            pltpu.VMEM((1, owned), F32),
            pltpu.VMEM((slots, 8 * owned, width), BF16),
            pltpu.VMEM((slots, rows, width), F32),
            pltpu.VMEM((slots, rows, width), F32),
            pltpu.VMEM((slots, rows, width), BF16),
            pltpu.VMEM((slots, 8, 128), F32),
            pltpu.VMEM((slots, 8, 128), F32),
            pltpu.VMEM((1, 8, 128), F32),
            pltpu.VMEM((slots, 8, 128), F32),
            dma, dma((6,)), dma((6,)), dma((6,)), dma, dma((3,)),
            dma((6,)), dma((6,)), dma((6,)), dma((6,)), dma((6,)), dma((6,)),
        ],
        compiler_params=pltpu.CompilerParams(
            collective_id=0, has_side_effects=True, vmem_limit_bytes=40 * 1024 * 1024
        ),
    )(residual, panel, face_block, deluxe_inv, basis, face_size, coarse_idx, coarse_scale)


def solution(mesh):
    placed = (
        P("gx", "gy", "gz", None, None, None),
        P("gx", "gy", "gz", None, None, None),
        P("gx", "gy", "gz", None, None, None),
        P("gx", "gy", "gz", None, None, None),
        P("gx", "gy", "gz", None, None, None),
        P("gx", "gy", "gz", None),
        P("gx", "gy", "gz", None, None),
        P("gx", "gy", "gz", None),
    )
    sizes = tuple(mesh.shape[name] for name in AXES)
    return jax.shard_map(
        functools.partial(on_device, sizes),
        mesh=mesh,
        in_specs=placed,
        out_specs=P("gx", "gy", "gz", None, None, None),
        check_vma=False,
    )
```

```python
import functools

import jax
import jax.numpy as jnp
from jax import lax
from jax.experimental import pallas as pl
from jax.experimental.pallas import tpu as pltpu
from jax.sharding import PartitionSpec as P

AXES = ("gx", "gy", "gz")
ORDER = (0, 1, 4, 5, 2, 3)
MESH = pl.DeviceIdType.MESH
F32 = jnp.float32
BF16 = jnp.bfloat16


def dot_nt(a, b):
    return lax.dot_general(a, b, (((1,), (1,)), ((), ())), preferred_element_type=F32)


def dot_nn(a, b):
    return lax.dot_general(a, b, (((1,), (0,)), ((), ())), preferred_element_type=F32)


def kernel(
    sizes,
    residual, panel, face_block, deluxe_inv, basis, size_ref, idx_ref, scale_ref,
    out_ref,
    res_v, pan_v, fb_v, inv_v, bas_v, size_s, idx_v, scale_v,
    expanded, applied, recv1, averaged, send2, recv2, send3, recv3,
    sem_res, sem_pan, sem_fb, sem_inv, sem_bas, sem_small,
    ssem1, rsem1, ssem2, rsem2, ssem3, rsem3,
):
    me = [lax.axis_index(name) for name in AXES]

    def neighbour(slot):
        axis = slot // 2
        step = 1 if slot % 2 == 0 else sizes[axis] - 1
        coords = list(me)
        coords[axis] = lax.rem(me[axis] + step, sizes[axis])
        return tuple(coords)

    barrier = pltpu.get_barrier_semaphore()
    for slot in range(6):
        pl.semaphore_signal(barrier, inc=1, device_id=neighbour(slot), device_id_type=MESH)

    def remote(src, dst, ssem, rsem, slot):
        return pltpu.make_async_remote_copy(
            src_ref=src.at[slot] if src.shape[0] == 6 else src.at[0],
            dst_ref=dst.at[slot ^ 1],
            send_sem=ssem.at[slot],
            recv_sem=rsem.at[slot ^ 1],
            device_id=neighbour(slot),
            device_id_type=MESH,
        )

    c_size = pltpu.make_async_copy(size_ref.at[0, 0], size_s, sem_small.at[0])
    c_idx = pltpu.make_async_copy(idx_ref, idx_v, sem_small.at[1])
    c_scale = pltpu.make_async_copy(scale_ref.at[0, 0], scale_v, sem_small.at[2])
    c_res = pltpu.make_async_copy(residual.at[0, 0, 0], res_v, sem_res)
    c_bas = pltpu.make_async_copy(basis.at[0, 0, 0], bas_v, sem_bas)
    c_pan = [pltpu.make_async_copy(panel.at[0, 0, 0, s], pan_v.at[s], sem_pan.at[s]) for s in range(6)]
    c_fb = [pltpu.make_async_copy(face_block.at[0, 0, 0, s], fb_v.at[s], sem_fb.at[s]) for s in range(6)]
    c_inv = [pltpu.make_async_copy(deluxe_inv.at[0, 0, 0, s], inv_v.at[s], sem_inv.at[s]) for s in range(6)]
    for copy in (c_size, c_idx, c_scale, c_res, c_bas):
        copy.start()
    for s in ORDER:
        c_pan[s].start()
        c_fb[s].start()
    for s in ORDER:
        c_inv[s].start()

    width = res_v.shape[-1]
    lane = lax.broadcasted_iota(jnp.int32, (1, width), 1)
    c_size.wait()
    live = [lane < size_s[0, s] for s in range(6)]

    c_idx.wait()
    c_bas.wait()
    row = lax.broadcasted_iota(jnp.int32, (256, 1), 0)
    unknown = (row & 31) + 32 * (row >> 7)
    for s in ORDER:
        onehot = jnp.where(unknown == idx_v[s], 1.0, 0.0).astype(BF16)
        expanded[s] = dot_nn(onehot, bas_v[s]).astype(BF16)

    c_res.wait()
    for k, s in enumerate(ORDER):
        c_pan[s].wait()
        masked = jnp.where(live[s], res_v[s].astype(F32), 0.0).astype(BF16)
        inner = dot_nt(masked, pan_v[s]).astype(BF16)
        through = dot_nn(inner, pan_v[s])
        c_fb[s].wait()
        value = dot_nt(masked, fb_v[s]) - through
        applied[s] = jnp.where(live[s], value, 0.0)
        if k == 0:
            pl.semaphore_wait(barrier, 6)
        remote(applied, recv1, ssem1, rsem1, s).start()

    group8 = lax.broadcasted_iota(jnp.int32, (8, 128), 1) >> 5

    def packed(wide):
        total = jnp.where(group8 == 0, wide[0:8], 0.0)
        for j in range(1, 4):
            total = jnp.where(group8 == j, wide[8 * j:8 * j + 8], total)
        return total

    def spread(tile):
        return jnp.concatenate([jnp.where(group8 == j, tile, 0.0) for j in range(4)], axis=0)

    own = jnp.zeros((8, 128), F32)
    for s in ORDER:
        remote(applied, recv1, ssem1, rsem1, s ^ 1).wait_recv()
        c_inv[s].wait()
        summed = (applied[s] + recv1[s]).astype(BF16)
        value = jnp.where(live[s], dot_nt(summed, inv_v[s]), 0.0).astype(BF16)
        averaged[s] = value
        split = dot_nt(value, expanded[s])
        own = own + packed(split[:, 0:128])
        send2[s] = packed(split[:, 128:256])
        remote(send2, recv2, ssem2, rsem2, s).start()

    c_scale.wait()
    scale = jnp.concatenate([scale_v[...]] * 4, axis=1)
    for s in ORDER:
        remote(send2, recv2, ssem2, rsem2, s ^ 1).wait_recv()
        own = own + recv2[s]
    correction = own * scale
    send3[0] = correction
    for s in ORDER:
        remote(send3, recv3, ssem3, rsem3, s).start()

    def halves(tile):
        high = tile.astype(BF16)
        return high, (tile - high.astype(F32)).astype(BF16)

    mine = spread(correction)
    for s in ORDER:
        remote(send3, recv3, ssem3, rsem3, s ^ 1).wait_recv()
        table = jnp.concatenate([mine, spread(recv3[s])], axis=1)
        high, low = halves(table)
        added = dot_nn(high, expanded[s]) + dot_nn(low, expanded[s])
        out_ref[0, 0, 0, s] = jnp.where(live[s], averaged[s].astype(F32) + added, 0.0).astype(BF16)

    for s in ORDER:
        remote(applied, recv1, ssem1, rsem1, s).wait_send()
        remote(send2, recv2, ssem2, rsem2, s).wait_send()
        remote(send3, recv3, ssem3, rsem3, s).wait_send()


def on_device(sizes, residual, panel, face_block, deluxe_inv, basis, face_size, coarse_idx, coarse_scale):
    slots, rows, width = residual.shape[3:]
    depth = panel.shape[4]
    entries = basis.shape[4]
    owned = coarse_scale.shape[-1]
    dma = pltpu.SemaphoreType.DMA
    operands = (residual, panel, face_block, deluxe_inv, basis, face_size, coarse_idx.reshape((slots, 1, entries)), coarse_scale)
    operands = [pltpu.with_memory_space_constraint(operand, pltpu.HBM) for operand in operands]
    return pl.pallas_call(
        functools.partial(kernel, sizes),
        out_shape=jax.ShapeDtypeStruct(residual.shape, BF16),
        in_specs=[pl.BlockSpec(memory_space=pl.ANY)] * 8,
        out_specs=pl.BlockSpec(memory_space=pltpu.VMEM),
        scratch_shapes=[
            pltpu.VMEM((slots, rows, width), BF16),
            pltpu.VMEM((slots, depth, width), BF16),
            pltpu.VMEM((slots, width, width), BF16),
            pltpu.VMEM((slots, width, width), BF16),
            pltpu.VMEM((slots, entries, width), BF16),
            pltpu.SMEM((1, slots), jnp.int32),
            pltpu.VMEM((slots, 1, entries), jnp.int32),
            pltpu.VMEM((1, owned), F32),
            pltpu.VMEM((slots, 8 * owned, width), BF16),
            pltpu.VMEM((slots, rows, width), F32),
            pltpu.VMEM((slots, rows, width), F32),
            pltpu.VMEM((slots, rows, width), BF16),
            pltpu.VMEM((slots, 8, 128), F32),
            pltpu.VMEM((slots, 8, 128), F32),
            pltpu.VMEM((1, 8, 128), F32),
            pltpu.VMEM((slots, 8, 128), F32),
            dma, dma((6,)), dma((6,)), dma((6,)), dma, dma((3,)),
            dma((6,)), dma((6,)), dma((6,)), dma((6,)), dma((6,)), dma((6,)),
        ],
        compiler_params=pltpu.CompilerParams(
            collective_id=0, has_side_effects=True, vmem_limit_bytes=32 * 1024 * 1024
        ),
    )(*operands)


def solution(mesh):
    placed = (
        P("gx", "gy", "gz", None, None, None),
        P("gx", "gy", "gz", None, None, None),
        P("gx", "gy", "gz", None, None, None),
        P("gx", "gy", "gz", None, None, None),
        P("gx", "gy", "gz", None, None, None),
        P("gx", "gy", "gz", None),
        P("gx", "gy", "gz", None, None),
        P("gx", "gy", "gz", None),
    )
    sizes = tuple(mesh.shape[name] for name in AXES)
    return jax.shard_map(
        functools.partial(on_device, sizes),
        mesh=mesh,
        in_specs=placed,
        out_specs=P("gx", "gy", "gz", None, None, None),
        check_vma=False,
    )
```

```python
import functools

import jax
import jax.numpy as jnp
from jax import lax
from jax.experimental import pallas as pl
from jax.experimental.pallas import tpu as pltpu
from jax.sharding import PartitionSpec as P

AXES = ("gx", "gy", "gz")
ORDER = (0, 1, 4, 5, 2, 3)
MESH = pl.DeviceIdType.MESH
F32 = jnp.float32
BF16 = jnp.bfloat16


def dot_nt(a, b):
    return lax.dot_general(a, b, (((1,), (1,)), ((), ())), preferred_element_type=F32)


def dot_nn(a, b):
    return lax.dot_general(a, b, (((1,), (0,)), ((), ())), preferred_element_type=F32)


def plan(sizes):
    def wrap(offset):
        return tuple(c % n for c, n in zip(offset, sizes))

    def plus(a, b):
        return wrap(tuple(x + y for x, y in zip(a, b)))

    units = []
    for slot in range(6):
        step = [0, 0, 0]
        step[slot // 2] = 1 if slot % 2 == 0 else -1
        units.append(wrap(step))
    near = list(dict.fromkeys(units))
    targets = {}
    for u in near:
        for d in [u] + [plus(u, t) for t in near]:
            if any(d):
                targets.setdefault(d, []).append(u)
    starts, total = {}, 0
    for d in targets:
        starts[d] = total
        total += 8 * (len(targets[d]) + (2 if d in near else 0))
    minus = lambda a, b: wrap(tuple(x - y for x, y in zip(a, b)))
    return units, near, targets, starts, total, minus


def kernel(
    sizes,
    residual, panel, face_block, deluxe_inv, basis, size_ref, idx_ref, scale_ref,
    out_ref,
    res_v, pan_v, fb_v, inv_v, bas_v, size_s, idx_v, scale_v,
    expanded, applied, recv1, averaged, send2, recv2,
    sem_res, sem_pan, sem_fb, sem_inv, sem_bas, sem_small,
    ssem1, rsem1, ssem2, rsem2,
):
    me = [lax.axis_index(name) for name in AXES]

    def neighbour(slot):
        axis = slot // 2
        step = 1 if slot % 2 == 0 else sizes[axis] - 1
        coords = list(me)
        coords[axis] = lax.rem(me[axis] + step, sizes[axis])
        return tuple(coords)

    units, near, targets, starts, _, minus = plan(sizes)

    def at_offset(offset):
        return tuple(lax.rem(m + c, n) for m, c, n in zip(me, offset, sizes))

    barrier = pltpu.get_barrier_semaphore()
    for d in targets:
        pl.semaphore_signal(barrier, inc=1, device_id=at_offset(d), device_id_type=MESH)

    def remote(src, dst, ssem, rsem, slot):
        return pltpu.make_async_remote_copy(
            src_ref=src.at[slot],
            dst_ref=dst.at[slot ^ 1],
            send_sem=ssem.at[slot],
            recv_sem=rsem.at[slot ^ 1],
            device_id=neighbour(slot),
            device_id_type=MESH,
        )

    c_size = pltpu.make_async_copy(size_ref.at[0, 0], size_s, sem_small.at[0])
    c_idx = pltpu.make_async_copy(idx_ref, idx_v, sem_small.at[1])
    c_scale = pltpu.make_async_copy(scale_ref.at[0, 0], scale_v, sem_small.at[2])
    c_res = pltpu.make_async_copy(residual.at[0, 0, 0], res_v, sem_res)
    c_bas = pltpu.make_async_copy(basis.at[0, 0, 0], bas_v, sem_bas)
    c_pan = [pltpu.make_async_copy(panel.at[0, 0, 0, s], pan_v.at[s], sem_pan.at[s]) for s in range(6)]
    c_fb = [pltpu.make_async_copy(face_block.at[0, 0, 0, s], fb_v.at[s], sem_fb.at[s]) for s in range(6)]
    c_inv = [pltpu.make_async_copy(deluxe_inv.at[0, 0, 0, s], inv_v.at[s], sem_inv.at[s]) for s in range(6)]
    for copy in (c_size, c_idx, c_scale, c_res, c_bas):
        copy.start()
    for s in ORDER:
        c_pan[s].start()
        c_fb[s].start()
    for s in ORDER:
        c_inv[s].start()

    width = res_v.shape[-1]
    lane = lax.broadcasted_iota(jnp.int32, (1, width), 1)
    c_size.wait()
    live = [lane < size_s[0, s] for s in range(6)]

    c_idx.wait()
    c_bas.wait()
    row = lax.broadcasted_iota(jnp.int32, (256, 1), 0)
    unknown = (row & 31) + 32 * (row >> 7)
    for s in ORDER:
        onehot = jnp.where(unknown == idx_v[s], 1.0, 0.0).astype(BF16)
        expanded[s] = dot_nn(onehot, bas_v[s]).astype(BF16)

    c_res.wait()
    for k, s in enumerate(ORDER):
        c_pan[s].wait()
        masked = jnp.where(live[s], res_v[s].astype(F32), 0.0).astype(BF16)
        inner = dot_nt(masked, pan_v[s]).astype(BF16)
        through = dot_nn(inner, pan_v[s])
        c_fb[s].wait()
        value = dot_nt(masked, fb_v[s]) - through
        applied[s] = jnp.where(live[s], value, 0.0)
        if k == 0:
            pl.semaphore_wait(barrier, len(targets))
        remote(applied, recv1, ssem1, rsem1, s).start()

    group8 = lax.broadcasted_iota(jnp.int32, (8, 128), 1) >> 5

    def packed(wide):
        total = jnp.where(group8 == 0, wide[0:8], 0.0)
        for j in range(1, 4):
            total = jnp.where(group8 == j, wide[8 * j:8 * j + 8], total)
        return total

    def spread(tile):
        return jnp.concatenate([jnp.where(group8 == j, tile, 0.0) for j in range(4)], axis=0)

    messages = []
    for i, d in enumerate(targets):
        rows = pl.ds(starts[d], 8 * (len(targets[d]) + (2 if d in near else 0)))
        messages.append(pltpu.make_async_remote_copy(
            src_ref=send2.at[rows],
            dst_ref=recv2.at[rows],
            send_sem=ssem2.at[i],
            recv_sem=rsem2.at[i],
            device_id=at_offset(d),
            device_id_type=MESH,
        ))

    c_scale.wait()
    scale = jnp.broadcast_to(jnp.concatenate([scale_v[...]] * 4, axis=1), (8, 128))
    own = jnp.zeros((8, 128), F32)
    outward = {}
    for s in ORDER:
        remote(applied, recv1, ssem1, rsem1, s ^ 1).wait_recv()
        c_inv[s].wait()
        summed = (applied[s] + recv1[s]).astype(BF16)
        value = jnp.where(live[s], dot_nt(summed, inv_v[s]), 0.0).astype(BF16)
        averaged[s] = value
        split = dot_nt(value, expanded[s])
        own = own + packed(split[:, 0:128])
        part = packed(split[:, 128:256])
        outward[units[s]] = outward[units[s]] + part if units[s] in outward else part
    for i, d in enumerate(targets):
        at = starts[d]
        for u in targets[d]:
            send2[pl.ds(at, 8)] = outward[u]
            at += 8
        if d in near:
            send2[pl.ds(at, 8)] = own
            send2[pl.ds(at + 8, 8)] = scale
        messages[i].start()

    zero = (0, 0, 0)
    coarse = dict(outward)
    coarse[zero] = own
    scales = {zero: scale}
    for i, d in enumerate(targets):
        messages[i].wait_recv()
        at = starts[d]
        for u in targets[d]:
            key = minus(u, d)
            coarse[key] = coarse[key] + recv2[pl.ds(at, 8)]
            at += 8
        if d in near:
            key = minus(zero, d)
            coarse[key] = coarse[key] + recv2[pl.ds(at, 8)]
            scales[key] = recv2[pl.ds(at + 8, 8)]
    correction = {key: coarse[key] * scales[key] for key in coarse}

    def halves(tile):
        high = tile.astype(BF16)
        return high, (tile - high.astype(F32)).astype(BF16)

    mine = spread(correction[zero])
    for s in ORDER:
        table = jnp.concatenate([mine, spread(correction[units[s]])], axis=1)
        high, low = halves(table)
        added = dot_nn(high, expanded[s]) + dot_nn(low, expanded[s])
        out_ref[0, 0, 0, s] = jnp.where(live[s], averaged[s].astype(F32) + added, 0.0).astype(BF16)

    for s in ORDER:
        remote(applied, recv1, ssem1, rsem1, s).wait_send()
    for message in messages:
        message.wait_send()


def on_device(sizes, residual, panel, face_block, deluxe_inv, basis, face_size, coarse_idx, coarse_scale):
    slots, rows, width = residual.shape[3:]
    depth = panel.shape[4]
    entries = basis.shape[4]
    owned = coarse_scale.shape[-1]
    dma = pltpu.SemaphoreType.DMA
    _, _, targets, _, total, _ = plan(sizes)
    count = len(targets)
    operands = (residual, panel, face_block, deluxe_inv, basis, face_size, coarse_idx.reshape((slots, 1, entries)), coarse_scale)
    operands = [pltpu.with_memory_space_constraint(operand, pltpu.HBM) for operand in operands]
    return pl.pallas_call(
        functools.partial(kernel, sizes),
        out_shape=jax.ShapeDtypeStruct(residual.shape, BF16),
        in_specs=[pl.BlockSpec(memory_space=pl.ANY)] * 8,
        out_specs=pl.BlockSpec(memory_space=pltpu.VMEM),
        scratch_shapes=[
            pltpu.VMEM((slots, rows, width), BF16),
            pltpu.VMEM((slots, depth, width), BF16),
            pltpu.VMEM((slots, width, width), BF16),
            pltpu.VMEM((slots, width, width), BF16),
            pltpu.VMEM((slots, entries, width), BF16),
            pltpu.SMEM((1, slots), jnp.int32),
            pltpu.VMEM((slots, 1, entries), jnp.int32),
            pltpu.VMEM((1, owned), F32),
            pltpu.VMEM((slots, 8 * owned, width), BF16),
            pltpu.VMEM((slots, rows, width), F32),
            pltpu.VMEM((slots, rows, width), F32),
            pltpu.VMEM((slots, rows, width), BF16),
            pltpu.VMEM((total, 128), F32),
            pltpu.VMEM((total, 128), F32),
            dma, dma((6,)), dma((6,)), dma((6,)), dma, dma((3,)),
            dma((6,)), dma((6,)), dma((count,)), dma((count,)),
        ],
        compiler_params=pltpu.CompilerParams(
            collective_id=0, has_side_effects=True, vmem_limit_bytes=32 * 1024 * 1024
        ),
    )(*operands)


def solution(mesh):
    placed = (
        P("gx", "gy", "gz", None, None, None),
        P("gx", "gy", "gz", None, None, None),
        P("gx", "gy", "gz", None, None, None),
        P("gx", "gy", "gz", None, None, None),
        P("gx", "gy", "gz", None, None, None),
        P("gx", "gy", "gz", None),
        P("gx", "gy", "gz", None, None),
        P("gx", "gy", "gz", None),
    )
    sizes = tuple(mesh.shape[name] for name in AXES)
    return jax.shard_map(
        functools.partial(on_device, sizes),
        mesh=mesh,
        in_specs=placed,
        out_specs=P("gx", "gy", "gz", None, None, None),
        check_vma=False,
    )
```

```python
import functools

import jax
import jax.numpy as jnp
from jax import lax
from jax.experimental import pallas as pl
from jax.experimental.pallas import tpu as pltpu
from jax.sharding import PartitionSpec as P

AXES = ("gx", "gy", "gz")
ORDER = (0, 1, 4, 5, 2, 3)
MESH = pl.DeviceIdType.MESH
F32 = jnp.float32
BF16 = jnp.bfloat16


def dot_nt(a, b):
    return lax.dot_general(a, b, (((1,), (1,)), ((), ())), preferred_element_type=F32)


def dot_nn(a, b):
    return lax.dot_general(a, b, (((1,), (0,)), ((), ())), preferred_element_type=F32)


def plan(sizes):
    def wrap(offset):
        return tuple(c % n for c, n in zip(offset, sizes))

    def plus(a, b):
        return wrap(tuple(x + y for x, y in zip(a, b)))

    units = []
    for slot in range(6):
        step = [0, 0, 0]
        step[slot // 2] = 1 if slot % 2 == 0 else -1
        units.append(wrap(step))
    near = list(dict.fromkeys(units))
    targets = {}
    for u in near:
        for d in [u] + [plus(u, t) for t in near]:
            if any(d):
                targets.setdefault(d, []).append(u)
    starts, total = {}, 0
    for d in targets:
        starts[d] = total
        total += 8 * (len(targets[d]) + (2 if d in near else 0))
    minus = lambda a, b: wrap(tuple(x - y for x, y in zip(a, b)))
    return units, near, targets, starts, total, minus


def kernel(
    sizes,
    residual, panel, face_block, deluxe_inv, basis, size_ref, idx_ref, scale_ref,
    out_ref,
    res_v, pan_v, fb_v, inv_v, bas_v, size_s, idx_v, scale_v,
    expanded, applied, recv1, averaged, send2, recv2,
    sem_res, sem_pan, sem_fb, sem_inv, sem_bas, sem_small,
    ssem1, rsem1, ssem2, rsem2,
):
    me = [lax.axis_index(name) for name in AXES]

    def neighbour(slot):
        axis = slot // 2
        step = 1 if slot % 2 == 0 else sizes[axis] - 1
        coords = list(me)
        coords[axis] = lax.rem(me[axis] + step, sizes[axis])
        return tuple(coords)

    units, near, targets, starts, _, minus = plan(sizes)

    def at_offset(offset):
        return tuple(lax.rem(m + c, n) for m, c, n in zip(me, offset, sizes))

    barrier = pltpu.get_barrier_semaphore()
    for d in targets:
        pl.semaphore_signal(barrier, inc=1, device_id=at_offset(d), device_id_type=MESH)

    def remote(src, dst, ssem, rsem, slot):
        return pltpu.make_async_remote_copy(
            src_ref=src.at[slot],
            dst_ref=dst.at[slot ^ 1],
            send_sem=ssem.at[slot],
            recv_sem=rsem.at[slot ^ 1],
            device_id=neighbour(slot),
            device_id_type=MESH,
        )

    c_size = pltpu.make_async_copy(size_ref.at[0, 0], size_s, sem_small.at[0])
    c_idx = pltpu.make_async_copy(idx_ref, idx_v, sem_small.at[1])
    c_scale = pltpu.make_async_copy(scale_ref.at[0, 0], scale_v, sem_small.at[2])
    c_res = pltpu.make_async_copy(residual.at[0, 0, 0], res_v, sem_res)
    c_bas = pltpu.make_async_copy(basis.at[0, 0, 0], bas_v, sem_bas)
    c_pan = [pltpu.make_async_copy(panel.at[0, 0, 0, s], pan_v.at[s], sem_pan.at[s]) for s in range(6)]
    c_fb = [pltpu.make_async_copy(face_block.at[0, 0, 0, s], fb_v.at[s], sem_fb.at[s]) for s in range(6)]
    c_inv = [pltpu.make_async_copy(deluxe_inv.at[0, 0, 0, s], inv_v.at[s], sem_inv.at[s]) for s in range(6)]
    for copy in (c_size, c_idx, c_scale, c_res, c_bas):
        copy.start()
    for s in ORDER:
        c_pan[s].start()
        c_fb[s].start()
    for s in ORDER:
        c_inv[s].start()

    width = res_v.shape[-1]
    lane = lax.broadcasted_iota(jnp.int32, (1, width), 1)
    c_size.wait()
    live = [lane < size_s[0, s] for s in range(6)]

    c_res.wait()
    for k, s in enumerate(ORDER):
        c_pan[s].wait()
        masked = jnp.where(live[s], res_v[s].astype(F32), 0.0).astype(BF16)
        inner = dot_nt(masked, pan_v[s]).astype(BF16)
        through = dot_nn(inner, pan_v[s])
        c_fb[s].wait()
        value = dot_nt(masked, fb_v[s]) - through
        applied[s] = jnp.where(live[s], value, 0.0)
        if k == 0:
            pl.semaphore_wait(barrier, len(targets))
        remote(applied, recv1, ssem1, rsem1, s).start()

    c_idx.wait()
    c_bas.wait()
    row = lax.broadcasted_iota(jnp.int32, (256, 1), 0)
    unknown = (row & 31) + 32 * (row >> 7)
    for s in ORDER:
        onehot = jnp.where(unknown == idx_v[s], 1.0, 0.0).astype(BF16)
        expanded[s] = dot_nn(onehot, bas_v[s]).astype(BF16)

    group8 = lax.broadcasted_iota(jnp.int32, (8, 128), 1) >> 5

    def packed(wide):
        total = jnp.where(group8 == 0, wide[0:8], 0.0)
        for j in range(1, 4):
            total = jnp.where(group8 == j, wide[8 * j:8 * j + 8], total)
        return total

    def spread(tile):
        return jnp.concatenate([jnp.where(group8 == j, tile, 0.0) for j in range(4)], axis=0)

    messages = []
    for i, d in enumerate(targets):
        rows = pl.ds(starts[d], 8 * (len(targets[d]) + (2 if d in near else 0)))
        messages.append(pltpu.make_async_remote_copy(
            src_ref=send2.at[rows],
            dst_ref=recv2.at[rows],
            send_sem=ssem2.at[i],
            recv_sem=rsem2.at[i],
            device_id=at_offset(d),
            device_id_type=MESH,
        ))

    c_scale.wait()
    scale = jnp.broadcast_to(jnp.concatenate([scale_v[...]] * 4, axis=1), (8, 128))
    own = jnp.zeros((8, 128), F32)
    outward = {}
    for s in ORDER:
        remote(applied, recv1, ssem1, rsem1, s ^ 1).wait_recv()
        c_inv[s].wait()
        summed = (applied[s] + recv1[s]).astype(BF16)
        value = jnp.where(live[s], dot_nt(summed, inv_v[s]), 0.0).astype(BF16)
        averaged[s] = value
        split = dot_nt(value, expanded[s])
        own = own + packed(split[:, 0:128])
        part = packed(split[:, 128:256])
        outward[units[s]] = outward[units[s]] + part if units[s] in outward else part
    for i, d in enumerate(targets):
        at = starts[d]
        for u in targets[d]:
            send2[pl.ds(at, 8)] = outward[u]
            at += 8
        if d in near:
            send2[pl.ds(at, 8)] = own
            send2[pl.ds(at + 8, 8)] = scale
        messages[i].start()

    zero = (0, 0, 0)
    coarse = dict(outward)
    coarse[zero] = own
    scales = {zero: scale}
    for i, d in enumerate(targets):
        messages[i].wait_recv()
        at = starts[d]
        for u in targets[d]:
            key = minus(u, d)
            coarse[key] = coarse[key] + recv2[pl.ds(at, 8)]
            at += 8
        if d in near:
            key = minus(zero, d)
            coarse[key] = coarse[key] + recv2[pl.ds(at, 8)]
            scales[key] = recv2[pl.ds(at + 8, 8)]
    correction = {key: coarse[key] * scales[key] for key in coarse}

    def halves(tile):
        high = tile.astype(BF16)
        return high, (tile - high.astype(F32)).astype(BF16)

    mine = spread(correction[zero])
    for s in ORDER:
        table = jnp.concatenate([mine, spread(correction[units[s]])], axis=1)
        high, low = halves(table)
        added = dot_nn(high, expanded[s]) + dot_nn(low, expanded[s])
        out_ref[0, 0, 0, s] = jnp.where(live[s], averaged[s].astype(F32) + added, 0.0).astype(BF16)

    for s in ORDER:
        remote(applied, recv1, ssem1, rsem1, s).wait_send()
    for message in messages:
        message.wait_send()


def on_device(sizes, residual, panel, face_block, deluxe_inv, basis, face_size, coarse_idx, coarse_scale):
    slots, rows, width = residual.shape[3:]
    depth = panel.shape[4]
    entries = basis.shape[4]
    owned = coarse_scale.shape[-1]
    dma = pltpu.SemaphoreType.DMA
    _, _, targets, _, total, _ = plan(sizes)
    count = len(targets)
    operands = (residual, panel, face_block, deluxe_inv, basis, face_size, coarse_idx.reshape((slots, 1, entries)), coarse_scale)
    operands = [pltpu.with_memory_space_constraint(operand, pltpu.HBM) for operand in operands]
    return pl.pallas_call(
        functools.partial(kernel, sizes),
        out_shape=jax.ShapeDtypeStruct(residual.shape, BF16),
        in_specs=[pl.BlockSpec(memory_space=pl.ANY)] * 8,
        out_specs=pl.BlockSpec(memory_space=pltpu.VMEM),
        scratch_shapes=[
            pltpu.VMEM((slots, rows, width), BF16),
            pltpu.VMEM((slots, depth, width), BF16),
            pltpu.VMEM((slots, width, width), BF16),
            pltpu.VMEM((slots, width, width), BF16),
            pltpu.VMEM((slots, entries, width), BF16),
            pltpu.SMEM((1, slots), jnp.int32),
            pltpu.VMEM((slots, 1, entries), jnp.int32),
            pltpu.VMEM((1, owned), F32),
            pltpu.VMEM((slots, 8 * owned, width), BF16),
            pltpu.VMEM((slots, rows, width), F32),
            pltpu.VMEM((slots, rows, width), F32),
            pltpu.VMEM((slots, rows, width), BF16),
            pltpu.VMEM((total, 128), F32),
            pltpu.VMEM((total, 128), F32),
            dma, dma((6,)), dma((6,)), dma((6,)), dma, dma((3,)),
            dma((6,)), dma((6,)), dma((count,)), dma((count,)),
        ],
        compiler_params=pltpu.CompilerParams(
            collective_id=0, has_side_effects=True, vmem_limit_bytes=32 * 1024 * 1024
        ),
    )(*operands)


def solution(mesh):
    placed = (
        P("gx", "gy", "gz", None, None, None),
        P("gx", "gy", "gz", None, None, None),
        P("gx", "gy", "gz", None, None, None),
        P("gx", "gy", "gz", None, None, None),
        P("gx", "gy", "gz", None, None, None),
        P("gx", "gy", "gz", None),
        P("gx", "gy", "gz", None, None),
        P("gx", "gy", "gz", None),
    )
    sizes = tuple(mesh.shape[name] for name in AXES)
    return jax.shard_map(
        functools.partial(on_device, sizes),
        mesh=mesh,
        in_specs=placed,
        out_specs=P("gx", "gy", "gz", None, None, None),
        check_vma=False,
    )
```

```python
import functools

import jax
import jax.numpy as jnp
from jax import lax
from jax.experimental import pallas as pl
from jax.experimental.pallas import tpu as pltpu
from jax.sharding import PartitionSpec as P

AXES = ("gx", "gy", "gz")
ORDER = (0, 1, 4, 5, 2, 3)
MESH = pl.DeviceIdType.MESH
F32 = jnp.float32
BF16 = jnp.bfloat16


def dot_nt(a, b):
    return lax.dot_general(a, b, (((1,), (1,)), ((), ())), preferred_element_type=F32)


def dot_nn(a, b):
    return lax.dot_general(a, b, (((1,), (0,)), ((), ())), preferred_element_type=F32)


def plan(sizes):
    def wrap(offset):
        return tuple(c % n for c, n in zip(offset, sizes))

    def plus(a, b):
        return wrap(tuple(x + y for x, y in zip(a, b)))

    units = []
    for slot in range(6):
        step = [0, 0, 0]
        step[slot // 2] = 1 if slot % 2 == 0 else -1
        units.append(wrap(step))
    near = list(dict.fromkeys(units))
    targets = {}
    for u in near:
        for d in [u] + [plus(u, t) for t in near]:
            if any(d):
                targets.setdefault(d, []).append(u)
    starts, total = {}, 0
    for d in targets:
        starts[d] = total
        total += 8 * (len(targets[d]) + (2 if d in near else 0))
    minus = lambda a, b: wrap(tuple(x - y for x, y in zip(a, b)))
    return units, near, targets, starts, total, minus


def kernel(
    sizes,
    residual, panel, face_block, deluxe_inv, basis, size_ref, idx_ref, scale_ref,
    out_ref,
    res_v, pan_v, fb_v, inv_v, bas_v, size_s, idx_v, scale_v,
    expanded, applied, recv1, averaged, send2, recv2,
    sem_res, sem_pan, sem_fb, sem_inv, sem_bas, sem_small,
    ssem1, rsem1, ssem2, rsem2,
):
    me = [lax.axis_index(name) for name in AXES]

    def neighbour(slot):
        axis = slot // 2
        step = 1 if slot % 2 == 0 else sizes[axis] - 1
        coords = list(me)
        coords[axis] = lax.rem(me[axis] + step, sizes[axis])
        return tuple(coords)

    units, near, targets, starts, _, minus = plan(sizes)

    def at_offset(offset):
        return tuple(lax.rem(m + c, n) for m, c, n in zip(me, offset, sizes))

    barrier = pltpu.get_barrier_semaphore()
    for d in targets:
        pl.semaphore_signal(barrier, inc=1, device_id=at_offset(d), device_id_type=MESH)

    def remote(src, dst, ssem, rsem, slot):
        return pltpu.make_async_remote_copy(
            src_ref=src.at[slot],
            dst_ref=dst.at[slot ^ 1],
            send_sem=ssem.at[slot],
            recv_sem=rsem.at[slot ^ 1],
            device_id=neighbour(slot),
            device_id_type=MESH,
        )

    c_size = pltpu.make_async_copy(size_ref.at[0, 0], size_s, sem_small.at[0])
    c_idx = pltpu.make_async_copy(idx_ref, idx_v, sem_small.at[1])
    c_scale = pltpu.make_async_copy(scale_ref.at[0, 0], scale_v, sem_small.at[2])
    c_res = pltpu.make_async_copy(residual.at[0, 0, 0], res_v, sem_res)
    c_bas = pltpu.make_async_copy(basis.at[0, 0, 0], bas_v, sem_bas)
    c_pan = [pltpu.make_async_copy(panel.at[0, 0, 0, s], pan_v.at[s], sem_pan.at[s]) for s in range(6)]
    c_fb = [pltpu.make_async_copy(face_block.at[0, 0, 0, s], fb_v.at[s], sem_fb.at[s]) for s in range(6)]
    c_inv = [pltpu.make_async_copy(deluxe_inv.at[0, 0, 0, s], inv_v.at[s], sem_inv.at[s]) for s in range(6)]
    for copy in (c_size, c_idx, c_scale, c_res, c_bas):
        copy.start()
    for s in ORDER:
        c_pan[s].start()
        c_fb[s].start()
    for s in ORDER:
        c_inv[s].start()

    width = res_v.shape[-1]
    lane = lax.broadcasted_iota(jnp.int32, (1, width), 1)
    c_size.wait()
    live = [lane < size_s[0, s] for s in range(6)]

    c_res.wait()
    for k, s in enumerate(ORDER):
        c_pan[s].wait()
        masked = jnp.where(live[s], res_v[s].astype(F32), 0.0).astype(BF16)
        inner = dot_nt(masked, pan_v[s]).astype(BF16)
        through = dot_nn(inner, pan_v[s])
        c_fb[s].wait()
        value = dot_nt(masked, fb_v[s]) - through
        applied[s] = jnp.where(live[s], value, 0.0)
        if k == 0:
            pl.semaphore_wait(barrier, len(targets))
        remote(applied, recv1, ssem1, rsem1, s).start()

    c_idx.wait()
    c_bas.wait()
    row = lax.broadcasted_iota(jnp.int32, (256, 1), 0)
    unknown = (row & 31) + 32 * (row >> 7)
    for s in ORDER:
        onehot = jnp.where(unknown == idx_v[s], 1.0, 0.0).astype(BF16)
        expanded[s] = dot_nn(onehot, bas_v[s]).astype(BF16)

    group8 = lax.broadcasted_iota(jnp.int32, (8, 128), 1) >> 5

    def packed(wide):
        total = jnp.where(group8 == 0, wide[0:8], 0.0)
        for j in range(1, 4):
            total = jnp.where(group8 == j, wide[8 * j:8 * j + 8], total)
        return total

    def spread(tile):
        return jnp.concatenate([jnp.where(group8 == j, tile, 0.0) for j in range(4)], axis=0)

    messages = []
    for i, d in enumerate(targets):
        rows = pl.ds(starts[d], 8 * (len(targets[d]) + (2 if d in near else 0)))
        messages.append(pltpu.make_async_remote_copy(
            src_ref=send2.at[rows],
            dst_ref=recv2.at[rows],
            send_sem=ssem2.at[i],
            recv_sem=rsem2.at[i],
            device_id=at_offset(d),
            device_id_type=MESH,
        ))

    c_scale.wait()
    scale = jnp.broadcast_to(jnp.concatenate([scale_v[...]] * 4, axis=1), (8, 128))
    own = jnp.zeros((8, 128), F32)
    outward = {}
    done, sent = [], []

    def send(i, d):
        at = starts[d]
        for u in targets[d]:
            send2[pl.ds(at, 8)] = outward[u]
            at += 8
        if d in near:
            send2[pl.ds(at, 8)] = own
            send2[pl.ds(at + 8, 8)] = scale
        messages[i].start()
        sent.append(d)

    for s in ORDER:
        remote(applied, recv1, ssem1, rsem1, s ^ 1).wait_recv()
        c_inv[s].wait()
        summed = (applied[s] + recv1[s]).astype(BF16)
        value = jnp.where(live[s], dot_nt(summed, inv_v[s]), 0.0).astype(BF16)
        averaged[s] = value
        split = dot_nt(value, expanded[s])
        own = own + packed(split[:, 0:128])
        part = packed(split[:, 128:256])
        outward[units[s]] = outward[units[s]] + part if units[s] in outward else part
        done.append(s)
        for i, d in enumerate(targets):
            ready = all(t in done for t in range(6) if units[t] in targets[d])
            if d not in sent and d not in near and ready:
                send(i, d)
    for i, d in enumerate(targets):
        if d not in sent:
            send(i, d)

    zero = (0, 0, 0)
    coarse = dict(outward)
    coarse[zero] = own
    scales = {zero: scale}
    for i, d in enumerate(targets):
        messages[i].wait_recv()
        at = starts[d]
        for u in targets[d]:
            key = minus(u, d)
            coarse[key] = coarse[key] + recv2[pl.ds(at, 8)]
            at += 8
        if d in near:
            key = minus(zero, d)
            coarse[key] = coarse[key] + recv2[pl.ds(at, 8)]
            scales[key] = recv2[pl.ds(at + 8, 8)]
    correction = {key: coarse[key] * scales[key] for key in coarse}

    def halves(tile):
        high = tile.astype(BF16)
        return high, (tile - high.astype(F32)).astype(BF16)

    mine = spread(correction[zero])
    for s in ORDER:
        table = jnp.concatenate([mine, spread(correction[units[s]])], axis=1)
        high, low = halves(table)
        both = dot_nn(jnp.concatenate([high, low], axis=0), expanded[s])
        rows = high.shape[0]
        added = both[0:rows] + both[rows:2 * rows]
        out_ref[0, 0, 0, s] = jnp.where(live[s], averaged[s].astype(F32) + added, 0.0).astype(BF16)

    for s in ORDER:
        remote(applied, recv1, ssem1, rsem1, s).wait_send()
    for message in messages:
        message.wait_send()


def on_device(sizes, residual, panel, face_block, deluxe_inv, basis, face_size, coarse_idx, coarse_scale):
    slots, rows, width = residual.shape[3:]
    depth = panel.shape[4]
    entries = basis.shape[4]
    owned = coarse_scale.shape[-1]
    dma = pltpu.SemaphoreType.DMA
    _, _, targets, _, total, _ = plan(sizes)
    count = len(targets)
    operands = (residual, panel, face_block, deluxe_inv, basis, face_size, coarse_idx.reshape((slots, 1, entries)), coarse_scale)
    operands = [pltpu.with_memory_space_constraint(operand, pltpu.HBM) for operand in operands]
    return pl.pallas_call(
        functools.partial(kernel, sizes),
        out_shape=jax.ShapeDtypeStruct(residual.shape, BF16),
        in_specs=[pl.BlockSpec(memory_space=pl.ANY)] * 8,
        out_specs=pl.BlockSpec(memory_space=pltpu.VMEM),
        scratch_shapes=[
            pltpu.VMEM((slots, rows, width), BF16),
            pltpu.VMEM((slots, depth, width), BF16),
            pltpu.VMEM((slots, width, width), BF16),
            pltpu.VMEM((slots, width, width), BF16),
            pltpu.VMEM((slots, entries, width), BF16),
            pltpu.SMEM((1, slots), jnp.int32),
            pltpu.VMEM((slots, 1, entries), jnp.int32),
            pltpu.VMEM((1, owned), F32),
            pltpu.VMEM((slots, 8 * owned, width), BF16),
            pltpu.VMEM((slots, rows, width), F32),
            pltpu.VMEM((slots, rows, width), F32),
            pltpu.VMEM((slots, rows, width), BF16),
            pltpu.VMEM((total, 128), F32),
            pltpu.VMEM((total, 128), F32),
            dma, dma((6,)), dma((6,)), dma((6,)), dma, dma((3,)),
            dma((6,)), dma((6,)), dma((count,)), dma((count,)),
        ],
        compiler_params=pltpu.CompilerParams(
            collective_id=0, has_side_effects=True, vmem_limit_bytes=32 * 1024 * 1024
        ),
    )(*operands)


def solution(mesh):
    placed = (
        P("gx", "gy", "gz", None, None, None),
        P("gx", "gy", "gz", None, None, None),
        P("gx", "gy", "gz", None, None, None),
        P("gx", "gy", "gz", None, None, None),
        P("gx", "gy", "gz", None, None, None),
        P("gx", "gy", "gz", None),
        P("gx", "gy", "gz", None, None),
        P("gx", "gy", "gz", None),
    )
    sizes = tuple(mesh.shape[name] for name in AXES)
    return jax.shard_map(
        functools.partial(on_device, sizes),
        mesh=mesh,
        in_specs=placed,
        out_specs=P("gx", "gy", "gz", None, None, None),
        check_vma=False,
    )
```
